32 devices in a mesh: slab: 8 (over y, x, core), cross: 4 (over z).
Axes of the slice: x: 2, y: 2, z: 4, core: 2. Of those that a mesh axis runs over, the one named last changes fastest.
Arguments:
- source: float32 [8, 4, 4, 16, 256], P('slab', None, 'cross'), may hold values from -75 to 75
- reaction: float32 [8, 4, 4, 16, 256], P('slab', None, 'cross'), may hold values from 0.05 to 3
- counts: int32 [8], replicated, may hold values from 1 to 4, 16 in all
- orientation: int32 [8, 4, 4], P('slab', None, 'cross'), may hold values from 0 to 3
Outputs:
- potential: float32 [8, 4, 4, 16, 256], P('slab', None, 'cross')
- velocity: float32 [3, 8, 4, 4, 16, 256], P(None, 'slab', None, 'cross')
The draws below stay inside these ranges and needn't reach their ends.
Inputs may be any that keep to these rules, and one draw needn't show every extreme that they name: counts sum to 16; the largest is 4.
All inputs are finite; a program needn't handle non-finite values.
Results may differ from the reference program's by a relative error of at most 0.0003.
Values sent between devices are 32-bit elements; how exact they have to be, the bound alone decides.
A program may use at most 64 MiB of HBM per device.

```python
import math
import jax
import jax.numpy as jnp
import numpy as np
from jax import lax

EDGE = 16
MEAN_MAC = 2
M_CAP = 4
ITERS = 2
LEVELS = 4
SWEEPS = 4
FLOW_MACROS = 16
N_SLAB = 8
N_CROSS = 4


def draw_source(key, part):
    key = jax.random.fold_in(key, 11)
    noise_key, scale_key = jax.random.split(key)
    shape = (N_SLAB, M_CAP, N_CROSS, EDGE, EDGE * EDGE)
    ramp = jnp.exp(jnp.log(3.0) * jnp.arange(N_SLAB, dtype=jnp.float32) / max(N_SLAB - 1, 1))
    noise = jnp.clip(jax.random.normal(noise_key, shape, jnp.float32), -6.0, 6.0)
    scales = jnp.exp(jax.random.uniform(scale_key, (N_SLAB, M_CAP, N_CROSS), jnp.float32, 0.0, jnp.log(3.0)))
    return noise * scales[..., None, None] * ramp[:, None, None, None, None]


def touch_ends(drawn, stream_key, low, high):
    shape = drawn.shape
    place = [jax.random.randint(jax.random.fold_in(stream_key, axis), (), 0, shape[axis]) for axis in range(len(shape))]
    drawn = drawn.at[tuple(place)].set(low)
    longest = shape.index(max(shape))
    place[longest] = (place[longest] + 1) % shape[longest]
    return drawn.at[tuple(place)].set(high)


def block_levels(own_key, dims, cuts, low, largest):
    gain, own = 1.0, jax.random.fold_in(own_key, 6)
    for dim, shards_of in cuts:
        steps = jnp.exp(jax.random.uniform(jax.random.fold_in(own, dim), (shards_of,), jnp.float32, low / len(cuts), largest / len(cuts)))
        gain = gain * jnp.repeat(steps, dims[dim] // shards_of).reshape([-1 if axis == dim else 1 for axis in range(len(dims))])
    return gain


def split_up(count, total, reach, slope):
    portions = [(1 << 20) // math.isqrt(standing ** slope) + 1 for standing in range(2, count + 1)]
    rest, given = total - reach - (count - 1), [1] * (count - 1)
    while rest > 0:
        candidates = [i for i in range(count - 1) if given[i] < reach]
        mass, budget = sum([portions[i] for i in candidates]), rest
        for i in candidates:
            addition = min(reach - given[i], max(1, budget * portions[i] // mass), rest)
            given[i] = given[i] + addition
            rest = rest - addition
    return np.array([reach] + given)


def ragged(stream_key, amount, total, reach, skew):
    if amount == 2:
        one = jax.random.randint(stream_key, (), max(1, total - reach), min(reach, total - 1) + 1)
        return jnp.stack([one, total - one])
    sizes = jnp.asarray(split_up(amount, total, reach, skew), jnp.int32)
    pairs = (amount - 1) // 2
    donor, receiver = sizes[1:1 + 2 * pairs:2], sizes[2:2 + 2 * pairs:2]
    slack = jnp.minimum(donor - 1, reach - receiver)
    passed = jax.random.randint(jax.random.fold_in(stream_key, 1), (pairs,), 0, 1 << 20) % (slack + 1)
    sizes = sizes.at[1:1 + 2 * pairs:2].set(donor - passed).at[2:2 + 2 * pairs:2].set(receiver + passed)
    return sizes[jax.random.permutation(jax.random.fold_in(stream_key, 2), amount)]


def setup_inputs(seed: int = 0) -> dict:
    seeds = jax.random.split(jax.random.key(seed), 5)
    source = draw_source(jax.random.fold_in(seeds[4], 71), 0)
    reaction = jnp.clip(jnp.exp(math.log(3.0) - 4.0943445 * jax.random.uniform(seeds[1], (N_SLAB, M_CAP, N_CROSS, EDGE, EDGE * EDGE), jnp.float32) ** block_levels(seeds[1], (N_SLAB, M_CAP, N_CROSS, EDGE, EDGE * EDGE), ((0, 8), (2, 4)), -0.2, 0.2)), 0.05, 3.0)
    counts = ragged(seeds[2], N_SLAB, MEAN_MAC * N_SLAB, M_CAP, 2).astype(jnp.int32)
    orientation = touch_ends(jax.random.randint(seeds[3], (N_SLAB, M_CAP, N_CROSS), 0, 4), jax.random.fold_in(seeds[3], 1), 0, 3).astype(jnp.int32)
    return {"source": source, "reaction": reaction, "counts": counts, "orientation": orientation}


DAMPING = 0.8


def rotate_in(local_cells, turn_codes):
    turned = turn_codes[..., None, None, None]
    swapped = jnp.swapaxes(local_cells, -3, -2)
    return jnp.where(turned == 0, local_cells, jnp.where(turned == 1, jnp.flip(swapped, -3), jnp.where(turned == 2, jnp.flip(local_cells, (-3, -2)), jnp.flip(swapped, -2))))


def rotate_out(placed, turn_codes):
    turned = turn_codes[..., None, None, None]
    swapped = jnp.swapaxes(placed, -3, -2)
    return jnp.where(turned == 0, placed, jnp.where(turned == 1, jnp.flip(swapped, -2), jnp.where(turned == 2, jnp.flip(placed, (-3, -2)), jnp.flip(swapped, -3))))


def positions(counts):
    starts = (jnp.cumsum(counts) - counts).astype(jnp.int32)
    slot_ids = jnp.arange(M_CAP, dtype=jnp.int32)
    alive_slot = slot_ids[None, :] < counts[:, None]
    return (starts[:, None] + slot_ids[None, :]).astype(jnp.int32), alive_slot


def assemble(field_slots, counts, orientation):
    macro_place, alive_slot = positions(counts)
    macro_place = jnp.where(alive_slot, macro_place, FLOW_MACROS).astype(jnp.int32)

    def turn_row(row_args):
        values, turn_codes = row_args
        return rotate_in(values.reshape(M_CAP, N_CROSS, EDGE, EDGE, EDGE), turn_codes)

    turned = lax.map(turn_row, (field_slots, orientation))
    macro_box = jnp.zeros((FLOW_MACROS, N_CROSS, EDGE, EDGE, EDGE), jnp.float32)
    return macro_box.at[macro_place.reshape(-1)].set(turned.reshape(-1, N_CROSS, EDGE, EDGE, EDGE), mode="drop")


def disassemble(macro_box, counts, orientation):
    macro_place, alive_slot = positions(counts)
    macro_place = jnp.where(alive_slot, macro_place, 0).astype(jnp.int32)

    def pick_row(row_args):
        where_row, alive_row, turn_codes = row_args
        local_cells = rotate_out(macro_box[where_row], turn_codes)
        kept = jnp.where(alive_row[:, None, None, None, None], local_cells, 0.0)
        return kept.reshape(M_CAP, N_CROSS, EDGE, EDGE * EDGE)

    return lax.map(pick_row, (macro_place, alive_slot, orientation))


def to_grid(macro_box):
    return macro_box.transpose(0, 2, 1, 3, 4).reshape(1, FLOW_MACROS * EDGE, N_CROSS * EDGE, EDGE)


def to_box(whole_grid):
    return whole_grid.reshape(FLOW_MACROS, EDGE, N_CROSS, EDGE, EDGE).transpose(0, 2, 1, 3, 4)


def neighbours(values):
    padded = jnp.pad(values, ((0, 0), (1, 1), (1, 1), (1, 1)))
    total = padded[:, 2:, 1:-1, 1:-1] + padded[:, :-2, 1:-1, 1:-1]
    total = total + padded[:, 1:-1, 2:, 1:-1] + padded[:, 1:-1, :-2, 1:-1]
    return total + padded[:, 1:-1, 1:-1, 2:] + padded[:, 1:-1, 1:-1, :-2]


def apply_global(field_box, coef_box):
    return (6.0 + coef_box) * field_box - to_box(neighbours(to_grid(field_box)))


def restrict(values):
    half_size = values.shape[-1] // 2
    return values.reshape(-1, half_size, 2, half_size, 2, half_size, 2).mean(axis=(2, 4, 6))


def prolong(values):
    return jnp.repeat(jnp.repeat(jnp.repeat(values, 2, 1), 2, 2), 2, 3)


def vcycle(forcing, coef_levels, level_index):
    coef_level = coef_levels[level_index]
    level_scale = 4.0 ** (-level_index)
    diagonal = 6.0 * level_scale + coef_level

    def level_apply(values):
        return (6.0 * values - neighbours(values)) * level_scale + coef_level * values

    if level_index == LEVELS - 1:
        correction = jnp.zeros_like(forcing)
        for sweep_index in range(SWEEPS):
            correction = correction + DAMPING * (forcing - level_apply(correction)) / diagonal
        return correction
    correction = DAMPING * forcing / diagonal
    coarse = vcycle(restrict(forcing - level_apply(correction)), coef_levels, level_index + 1)
    correction = correction + prolong(coarse)
    return correction + DAMPING * (forcing - level_apply(correction)) / diagonal


def precondition(values, coef_levels):
    return vcycle(values.reshape(-1, EDGE, EDGE, EDGE), coef_levels, 0).reshape(values.shape)


def reference(source, reaction, counts, orientation):
    right_side = assemble(source, counts, orientation)
    coef_box = assemble(reaction, counts, orientation)
    coef_levels = [coef_box.reshape(-1, EDGE, EDGE, EDGE)]
    for level_index in range(LEVELS - 1):
        coef_levels.append(restrict(coef_levels[-1]))
    solution = jnp.zeros_like(right_side)
    residual = right_side
    smoothed = precondition(residual, coef_levels)
    direction = smoothed
    inner_now = jnp.sum(residual * smoothed)
    for iteration in range(ITERS):
        image_vec = apply_global(direction, coef_box)
        step_size = inner_now / jnp.sum(direction * image_vec)
        solution = solution + step_size * direction
        if iteration + 1 < ITERS:
            residual = residual - step_size * image_vec
            smoothed = precondition(residual, coef_levels)
            inner_next = jnp.sum(residual * smoothed)
            direction = smoothed + (inner_next / inner_now) * direction
            inner_now = inner_next
    padded = jnp.pad(to_grid(solution)[0], 1)
    along_x = 0.5 * (padded[2:, 1:-1, 1:-1] - padded[:-2, 1:-1, 1:-1])
    along_y = 0.5 * (padded[1:-1, 2:, 1:-1] - padded[1:-1, :-2, 1:-1])
    along_w = 0.5 * (padded[1:-1, 1:-1, 2:] - padded[1:-1, 1:-1, :-2])
    local_x = disassemble(to_box(along_x), counts, orientation)
    local_y = disassemble(to_box(along_y), counts, orientation)
    local_w = disassemble(to_box(along_w), counts, orientation)
    turn_codes = orientation[..., None, None]
    speed_u = jnp.where(turn_codes == 0, local_x, jnp.where(turn_codes == 1, local_y, jnp.where(turn_codes == 2, -local_x, -local_y)))
    speed_v = jnp.where(turn_codes == 0, local_y, jnp.where(turn_codes == 1, -local_x, jnp.where(turn_codes == 2, -local_y, local_x)))
    potential = disassemble(solution, counts, orientation)
    return potential, jnp.stack([speed_u, speed_v, local_w])
```

```python
import functools

import jax
import jax.numpy as jnp
from jax import lax
from jax.experimental import pallas as pl
from jax.experimental.pallas import tpu as pltpu
from jax.sharding import PartitionSpec as P

LEVELS = 4
SWEEPS = 4
DAMPING = 0.8
KEEP = 1.0 - DAMPING


def roll(x, shift, axis):
    return pltpu.roll(x, shift % x.shape[axis], axis)


def iota(shape, axis):
    return lax.broadcasted_iota(jnp.int32, shape, axis)


def keep(mask, x):
    return jnp.where(mask, x, 0.0)


class Grid:
    def __init__(self):
        self.u = iota((128, 128), 0) % 16
        self.w = iota((128, 128), 1) % 16
        self.g = iota((64, 128), 1) // 16
        self.gg = iota((128, 128), 1) // 16

    def shifts(self, x, d):
        prev_u = keep(self.u >= d, roll(x, d, 0))
        next_u = keep(self.u < 16 - d, roll(x, -d, 0))
        prev_w = keep(self.w >= d, roll(x, d, 1))
        next_w = keep(self.w < 16 - d, roll(x, -d, 1))
        up = roll(x, 16 * d, 1)
        down = roll(x, -16 * d, 1)
        inside = self.g >= d
        prev_v = jnp.concatenate([keep(inside, up[:64]), jnp.where(inside, up[64:], up[:64])], 0)
        inside = self.g < 8 - d
        next_v = jnp.concatenate([jnp.where(inside, down[:64], down[64:]), keep(inside, down[64:])], 0)
        return prev_u, next_u, prev_v, next_v, prev_w, next_w

    def near(self, x, d):
        if d == 8:
            swap_u = x.reshape(8, 2, 8, 128)
            swap_u = jnp.concatenate([swap_u[:, 1:], swap_u[:, :1]], 1).reshape(128, 128)
            swap_v = jnp.concatenate([x[64:], x[:64]], 0)
            swap_w = jnp.where(self.w >= 8, roll(x, 8, 1), roll(x, -8, 1))
            return swap_u + swap_v + swap_w
        prev_u, next_u, prev_v, next_v, prev_w, next_w = self.shifts(x, d)
        return (prev_u + next_u) + (prev_v + next_v) + (prev_w + next_w)

    def restrict(self, x, d):
        x = x + jnp.where((self.u & d) != 0, roll(x, d, 0), roll(x, -d, 0))
        if d == 4:
            x = x + roll(x, 64, 1)
        else:
            x = x + jnp.where((self.gg & d) != 0, roll(x, 16 * d, 1), roll(x, -16 * d, 1))
        x = x + jnp.where((self.w & d) != 0, roll(x, d, 1), roll(x, -d, 1))
        return x * 0.125


def vcycle(grid, f, inverse, level):
    d = 2**level
    scale = 4.0**-level
    inv = inverse[level]
    e = inv * f
    if level == LEVELS - 1:
        for _ in range(SWEEPS - 1):
            e = KEEP * e + inv * (f + scale * grid.near(e, d))
        return e
    e = e + vcycle(grid, grid.restrict(KEEP * f + scale * grid.near(e, d), d), inverse, level + 1)
    return KEEP * e + inv * (f + scale * grid.near(e, d))


def fold(x):
    return x.reshape(8, 8, 128).sum(1)


def unfold(x):
    return jnp.broadcast_to(x[:, None, :], (8, 8, 128)).reshape(64, 128)


def spread(x):
    x = x + roll(x, 16, 1)
    x = x + roll(x, 32, 1)
    return x + roll(x, 64, 1)


def flip(x):
    row = iota(x.shape, 0)
    group = iota(x.shape, 1) // 16
    x = jnp.where(row % 2 == 1, roll(x, 1, 0), roll(x, -1, 0))
    x = roll(x, 64, 1)
    x = jnp.where((group & 2) != 0, roll(x, 32, 1), roll(x, -32, 1))
    return jnp.where((group & 1) != 0, roll(x, 16, 1), roll(x, -16, 1))


def pick(turn, a, b, c, d):
    return jnp.where(turn == 0, a, jnp.where(turn == 1, b, jnp.where(turn == 2, c, d)))


def kernel(
    n_slab, n_cross, counts_ref, turn_ref, source_ref, reaction_ref, pot_ref, vel_ref,
    out_face, in_face, face_send, face_recv, mine, sums, sum_send, sum_recv,
    mine_z, sums_z, sum_send_z, sum_recv_z,
):
    slab = lax.axis_index("slab")
    cross = lax.axis_index("cross")

    in_face[...] = jnp.zeros_like(in_face)
    barrier = pltpu.get_barrier_semaphore()

    def each(count, body):
        if count <= 8:
            for step in range(1, count):
                body(step)
        else:
            lax.fori_loop(1, count, lambda step, carry: (body(step), carry)[1], 0)

    def greet_slab(step):
        pl.semaphore_signal(barrier, inc=1, device_id=(lax.rem(slab + step, n_slab), cross), device_id_type=pl.DeviceIdType.MESH)

    def greet_cross(step):
        pl.semaphore_signal(barrier, inc=1, device_id=(slab, lax.rem(cross + step, n_cross)), device_id_type=pl.DeviceIdType.MESH)

    each(n_slab, greet_slab)
    each(n_cross, greet_cross)

    grid = Grid()
    live = counts_ref[slab]
    row8 = iota((8, 128), 0)
    turn = jnp.where(row8 < 2, turn_ref[0], jnp.where(row8 < 4, turn_ref[1], jnp.where(row8 < 6, turn_ref[2], turn_ref[3])))
    alive = (iota((128, 128), 0) % 64) // 16 < live
    u64 = grid.u[:64]
    diagonal_face = u64 % 8 == grid.g

    def load(ref):
        x = ref[...]
        return jnp.concatenate([x[:, :128], x[:, 128:]], 0)

    r0 = keep(alive, load(source_ref))
    coef = jnp.where(alive, load(reaction_ref), 1.0)
    inverse = []
    level_coef = coef
    for level in range(LEVELS):
        inverse.append(DAMPING / (6.0 * 4.0**-level + level_coef))
        if level + 1 < LEVELS:
            level_coef = grid.restrict(level_coef, 2**level)

    def faces(x):
        lo, hi = x[:64], x[64:]
        u0 = fold(keep(u64 == 0, lo)) + roll(fold(keep(u64 == 0, hi)), 1, 0)
        u1 = roll(fold(keep(u64 == 15, lo)), -1, 0) + fold(keep(u64 == 15, hi))
        v0 = fold(keep(diagonal_face, spread(keep(grid.g == 0, lo))))
        v1 = fold(keep(diagonal_face, spread(keep(grid.g == 7, hi))))
        flipped = flip(jnp.concatenate([u0, u1, v0, v1], 0))
        fu0, fu1, fv0, fv1 = flipped[:8], flipped[8:16], flipped[16:24], flipped[24:]
        return (
            pick(turn, u0, v1, fu1, fv0),
            pick(turn, u1, v0, fu0, fv1),
            pick(turn, v0, fu0, fv1, u1),
            pick(turn, v1, fu1, fv0, u0),
        )

    sides = (
        (slab + 1 < n_slab, slab > 0, (slab + 1, cross)),
        (slab > 0, slab + 1 < n_slab, (slab - 1, cross)),
        (cross + 1 < n_cross, cross > 0, (slab, cross + 1)),
        (cross > 0, cross + 1 < n_cross, (slab, cross - 1)),
    )

    def face_copy(turn_of, side):
        return pltpu.make_async_remote_copy(
            src_ref=out_face.at[turn_of, side],
            dst_ref=in_face.at[turn_of, side],
            send_sem=face_send.at[turn_of, side],
            recv_sem=face_recv.at[turn_of, side],
            device_id=sides[side][2],
            device_id_type=pl.DeviceIdType.MESH,
        )

    def exchange_start(turn_of, x):
        x0, x1, y0, y1 = faces(x)
        last = jnp.where(live == 1, x1, jnp.where(live == 2, roll(x1, -2, 0), jnp.where(live == 3, roll(x1, -4, 0), roll(x1, -6, 0))))
        out_face[turn_of, 0] = last
        out_face[turn_of, 1] = x0
        out_face[turn_of, 2] = y1
        out_face[turn_of, 3] = y0
        for side in range(4):
            @pl.when(sides[side][0])
            def _():
                face_copy(turn_of, side).start()
        return x0, x1

    def exchange_end(turn_of, x0, x1):
        for side in range(4):
            @pl.when(sides[side][1])
            def _():
                face_copy(turn_of, side).wait_recv()
        right = keep(row8 < 2, in_face[turn_of, 1])
        right = right + roll(right, 2, 0)
        right = right + roll(right, 4, 0)
        gx0 = jnp.where(row8 < 2, in_face[turn_of, 0], roll(x1, 2, 0))
        gx1 = jnp.where(row8 < 2 * (live - 1), roll(x0, -2, 0), right)
        gy0 = in_face[turn_of, 2]
        gy1 = in_face[turn_of, 3]
        flipped = flip(jnp.concatenate([gx0, gx1, gy0, gy1], 0))
        fx0, fx1, fy0, fy1 = flipped[:8], flipped[8:16], flipped[16:24], flipped[24:]
        gu0 = pick(turn, gx0, fy0, fx1, gy1)
        gu1 = pick(turn, gx1, fy1, fx0, gy0)
        gv0 = pick(turn, gy0, gx1, fy1, fx0)
        gv1 = pick(turn, gy1, gx0, fy0, fx1)
        lo = jnp.where(u64 == 0, unfold(gu0), keep(u64 == 15, unfold(roll(gu1, 1, 0))))
        hi = jnp.where(u64 == 0, unfold(roll(gu0, -1, 0)), keep(u64 == 15, unfold(gu1)))
        rim_u = jnp.concatenate([lo, hi], 0)
        lo = keep(grid.g == 0, spread(keep(diagonal_face, unfold(gv0))))
        hi = keep(grid.g == 7, spread(keep(diagonal_face, unfold(gv1))))
        rim_v = jnp.concatenate([lo, hi], 0)
        return rim_u, rim_v

    def operate(x, rim_u, rim_v):
        return keep(alive, (6.0 + coef) * x - (grid.near(x, 1) + (rim_u + rim_v)))

    def inner(a, b):
        return (a * b).reshape(16, 8, 128).sum(0)

    z0 = vcycle(grid, r0, inverse, 0)
    pl.semaphore_wait(barrier, n_slab - 1 + n_cross - 1)
    z_faces = exchange_start(0, z0)
    dot_rz = inner(r0, z0)
    z_rims = exchange_end(0, *z_faces)
    q0 = operate(z0, *z_rims)
    w0 = vcycle(grid, q0, inverse, 0)
    w_faces = exchange_start(1, w0)
    dot_zq = inner(z0, q0)
    dot_rw = inner(r0, w0)
    dot_qw = inner(q0, w0)
    w_rims = exchange_end(1, *w_faces)
    dot_wv = inner(w0, operate(w0, *w_rims))
    none = jnp.zeros((8, 128), jnp.float32)
    partial = jnp.concatenate([dot_rz, dot_zq, dot_rw, dot_qw, dot_wv, none, none, none], 0)
    partial = partial.reshape(8, 8, 128).sum(1)

    def total(value, own, count, me, out, into, send, recv, place):
        out[...] = value

        def copy(source, target):
            return pltpu.make_async_remote_copy(
                src_ref=out, dst_ref=into.at[source], send_sem=send.at[target], recv_sem=recv.at[source],
                device_id=place(target), device_id_type=pl.DeviceIdType.MESH,
            )

        def begin(step):
            copy(me, lax.rem(me + step, count)).start()

        def arrive(step):
            copy(lax.rem(me + step, count), lax.rem(me + step, count)).wait_recv()

        def leave(step):
            copy(me, lax.rem(me + step, count)).wait_send()

        each(count, begin)
        into[me] = value
        each(count, arrive)
        result = into[...].sum(0)
        return result, lambda: each(count, leave)

    across, leave_slab = total(partial, slab, n_slab, slab, mine, sums, sum_send, sum_recv, lambda k: (k, cross))
    whole, leave_cross = total(across, cross, n_cross, cross, mine_z, sums_z, sum_send_z, sum_recv_z, lambda k: (slab, k))
    whole = jnp.sum(whole, 1, keepdims=True)
    rz, zq, rw, qw, wv = (whole[k : k + 1] for k in range(5))
    alpha = rz / zq
    rz_new = rz - alpha * (zq + rw) + alpha * alpha * qw
    gain = 1.0 + rz_new / rz
    pq = gain * gain * zq - 2.0 * gain * alpha * qw + alpha * alpha * wv
    step = rz_new / pq
    of_z = alpha + step * gain
    of_w = -step * alpha
    x = of_z * z0 + of_w * w0
    rim_u = of_z * z_rims[0] + of_w * w_rims[0]
    rim_v = of_z * z_rims[1] + of_w * w_rims[1]
    prev_u, next_u, prev_v, next_v, prev_w, next_w = grid.shifts(x, 1)
    rim_u = jnp.where(grid.u == 0, -rim_u, rim_u)
    rim_v = jnp.concatenate([-rim_v[:64], rim_v[64:]], 0)

    def store(ref, value):
        ref[...] = jnp.concatenate([value[:64], value[64:]], 1)

    store(pot_ref, x)
    store(vel_ref.at[0], keep(alive, 0.5 * (next_u - prev_u + rim_u)))
    store(vel_ref.at[1], keep(alive, 0.5 * (next_v - prev_v + rim_v)))
    store(vel_ref.at[2], keep(alive, 0.5 * (next_w - prev_w)))

    leave_slab()
    leave_cross()
    for turn_of in range(2):
        for side in range(4):
            @pl.when(sides[side][0])
            def _():
                face_copy(turn_of, side).wait_send()


def local(n_slab, n_cross, source, reaction, counts, orientation):
    slots, length = source.shape[1], source.shape[3]
    rows, lanes = slots * length, length * length
    dma = pltpu.SemaphoreType.DMA
    vmem = pl.BlockSpec(memory_space=pltpu.VMEM)
    smem = pl.BlockSpec(memory_space=pltpu.SMEM)
    potential, velocity = pl.pallas_call(
        functools.partial(kernel, n_slab, n_cross),
        out_shape=(
            jax.ShapeDtypeStruct((rows, lanes), jnp.float32),
            jax.ShapeDtypeStruct((3, rows, lanes), jnp.float32),
        ),
        in_specs=[smem, smem, vmem, vmem],
        out_specs=(vmem, vmem),
        scratch_shapes=[
            pltpu.VMEM((2, 4, 8, 128), jnp.float32),
            pltpu.VMEM((2, 4, 8, 128), jnp.float32),
            dma((2, 4)),
            dma((2, 4)),
            pltpu.VMEM((8, 128), jnp.float32),
            pltpu.VMEM((n_slab, 8, 128), jnp.float32),
            dma((n_slab,)),
            dma((n_slab,)),
            pltpu.VMEM((8, 128), jnp.float32),
            pltpu.VMEM((n_cross, 8, 128), jnp.float32),
            dma((n_cross,)),
            dma((n_cross,)),
        ],
        compiler_params=pltpu.CompilerParams(
            collective_id=0, has_side_effects=True, vmem_limit_bytes=16 * 2**20
        ),
    )(counts, orientation.reshape(slots), source.reshape(rows, lanes), reaction.reshape(rows, lanes))
    return potential.reshape(source.shape), velocity.reshape((3,) + source.shape)


def solution(mesh):
    spec = P("slab", None, "cross", None, None)
    return jax.shard_map(
        functools.partial(local, mesh.shape["slab"], mesh.shape["cross"]),
        mesh=mesh,
        in_specs=(spec, spec, P(), P("slab", None, "cross")),
        out_specs=(spec, P(None, "slab", None, "cross", None, None)),
        check_vma=False,
    )
```

```python
import functools

import jax
import jax.numpy as jnp
from jax import lax
from jax.experimental import pallas as pl
from jax.experimental.pallas import tpu as pltpu
from jax.sharding import PartitionSpec as P

LEVELS = 4
SWEEPS = 4
DAMPING = 0.8
KEEP = 1.0 - DAMPING


def roll(x, shift, axis):
    return pltpu.roll(x, shift % x.shape[axis], axis)


def iota(shape, axis):
    return lax.broadcasted_iota(jnp.int32, shape, axis)


def keep(mask, x):
    return jnp.where(mask, x, 0.0)


class Grid:
    def __init__(self):
        self.u = iota((128, 128), 0) % 16
        self.w = iota((128, 128), 1) % 16
        self.g = iota((64, 128), 1) // 16
        self.gg = iota((128, 128), 1) // 16

    def shifts(self, x, d):
        prev_u = keep(self.u >= d, roll(x, d, 0))
        next_u = keep(self.u < 16 - d, roll(x, -d, 0))
        prev_w = keep(self.w >= d, roll(x, d, 1))
        next_w = keep(self.w < 16 - d, roll(x, -d, 1))
        up = roll(x, 16 * d, 1)
        down = roll(x, -16 * d, 1)
        inside = self.g >= d
        prev_v = jnp.concatenate([keep(inside, up[:64]), jnp.where(inside, up[64:], up[:64])], 0)
        inside = self.g < 8 - d
        next_v = jnp.concatenate([jnp.where(inside, down[:64], down[64:]), keep(inside, down[64:])], 0)
        return prev_u, next_u, prev_v, next_v, prev_w, next_w

    def near(self, x, d):
        if d == 8:
            swap_u = x.reshape(8, 2, 8, 128)
            swap_u = jnp.concatenate([swap_u[:, 1:], swap_u[:, :1]], 1).reshape(128, 128)
            swap_v = jnp.concatenate([x[64:], x[:64]], 0)
            swap_w = jnp.where(self.w >= 8, roll(x, 8, 1), roll(x, -8, 1))
            return swap_u + swap_v + swap_w
        prev_u, next_u, prev_v, next_v, prev_w, next_w = self.shifts(x, d)
        return (prev_u + next_u) + (prev_v + next_v) + (prev_w + next_w)

    def restrict(self, x, d):
        x = x + jnp.where((self.u & d) != 0, roll(x, d, 0), roll(x, -d, 0))
        if d == 4:
            x = x + roll(x, 64, 1)
        else:
            x = x + jnp.where((self.gg & d) != 0, roll(x, 16 * d, 1), roll(x, -16 * d, 1))
        x = x + jnp.where((self.w & d) != 0, roll(x, d, 1), roll(x, -d, 1))
        return x * 0.125


def vcycle(grid, f, inverse, level):
    d = 2**level
    scale = 4.0**-level
    inv = inverse[level]
    e = inv * f
    if level == LEVELS - 1:
        for _ in range(SWEEPS - 1):
            e = KEEP * e + inv * (f + scale * grid.near(e, d))
        return e
    e = e + vcycle(grid, grid.restrict(KEEP * f + scale * grid.near(e, d), d), inverse, level + 1)
    return KEEP * e + inv * (f + scale * grid.near(e, d))


def fold(x):
    return x.reshape(8, 8, 128).sum(1)


def unfold(x):
    return jnp.broadcast_to(x[:, None, :], (8, 8, 128)).reshape(64, 128)


def spread(x):
    x = x + roll(x, 16, 1)
    x = x + roll(x, 32, 1)
    return x + roll(x, 64, 1)


def flip(x):
    row = iota(x.shape, 0)
    group = iota(x.shape, 1) // 16
    x = jnp.where(row % 2 == 1, roll(x, 1, 0), roll(x, -1, 0))
    x = roll(x, 64, 1)
    x = jnp.where((group & 2) != 0, roll(x, 32, 1), roll(x, -32, 1))
    return jnp.where((group & 1) != 0, roll(x, 16, 1), roll(x, -16, 1))


def pick(turn, a, b, c, d):
    return jnp.where(turn == 0, a, jnp.where(turn == 1, b, jnp.where(turn == 2, c, d)))


def kernel(
    n_slab, n_cross, counts_hbm, turn_hbm, source_hbm, reaction_hbm, pot_ref, vel_ref,
    counts_ref, turn_ref, source_ref, reaction_ref, load_sem,
    out_face, in_face, face_send, face_recv, mine, sums, sum_send, sum_recv,
    mine_z, sums_z, sum_send_z, sum_recv_z,
):
    slab = lax.axis_index("slab")
    cross = lax.axis_index("cross")

    loads = []
    pairs = ((counts_hbm, counts_ref), (reaction_hbm, reaction_ref), (turn_hbm, turn_ref), (source_hbm, source_ref))
    for place, (there, here) in enumerate(pairs):
        loads.append(pltpu.make_async_copy(there, here, load_sem.at[place]))
        loads[-1].start()

    in_face[...] = jnp.zeros_like(in_face)
    barrier = pltpu.get_barrier_semaphore()

    def each(count, body):
        if count <= 8:
            for step in range(1, count):
                body(step)
        else:
            lax.fori_loop(1, count, lambda step, carry: (body(step), carry)[1], 0)

    def greet_slab(step):
        pl.semaphore_signal(barrier, inc=1, device_id=(lax.rem(slab + step, n_slab), cross), device_id_type=pl.DeviceIdType.MESH)

    def greet_cross(step):
        pl.semaphore_signal(barrier, inc=1, device_id=(slab, lax.rem(cross + step, n_cross)), device_id_type=pl.DeviceIdType.MESH)

    each(n_slab, greet_slab)
    each(n_cross, greet_cross)

    grid = Grid()
    for each_load in loads:
        each_load.wait()
    live = counts_ref[slab]
    row8 = iota((8, 128), 0)
    turn = jnp.where(row8 < 2, turn_ref[0], jnp.where(row8 < 4, turn_ref[1], jnp.where(row8 < 6, turn_ref[2], turn_ref[3])))
    alive = (iota((128, 128), 0) % 64) // 16 < live
    u64 = grid.u[:64]
    diagonal_face = u64 % 8 == grid.g

    def load(ref):
        x = ref[...]
        return jnp.concatenate([x[:, :128], x[:, 128:]], 0)

    r0 = keep(alive, load(source_ref))
    coef = jnp.where(alive, load(reaction_ref), 1.0)
    inverse = []
    level_coef = coef
    for level in range(LEVELS):
        inverse.append(DAMPING / (6.0 * 4.0**-level + level_coef))
        if level + 1 < LEVELS:
            level_coef = grid.restrict(level_coef, 2**level)

    def faces(x):
        lo, hi = x[:64], x[64:]
        u0 = fold(keep(u64 == 0, lo)) + roll(fold(keep(u64 == 0, hi)), 1, 0)
        u1 = roll(fold(keep(u64 == 15, lo)), -1, 0) + fold(keep(u64 == 15, hi))
        v0 = fold(keep(diagonal_face, spread(keep(grid.g == 0, lo))))
        v1 = fold(keep(diagonal_face, spread(keep(grid.g == 7, hi))))
        flipped = flip(jnp.concatenate([u0, u1, v0, v1], 0))
        fu0, fu1, fv0, fv1 = flipped[:8], flipped[8:16], flipped[16:24], flipped[24:]
        return (
            pick(turn, u0, v1, fu1, fv0),
            pick(turn, u1, v0, fu0, fv1),
            pick(turn, v0, fu0, fv1, u1),
            pick(turn, v1, fu1, fv0, u0),
        )

    sides = (
        (slab + 1 < n_slab, slab > 0, (slab + 1, cross)),
        (slab > 0, slab + 1 < n_slab, (slab - 1, cross)),
        (cross + 1 < n_cross, cross > 0, (slab, cross + 1)),
        (cross > 0, cross + 1 < n_cross, (slab, cross - 1)),
    )

    def face_copy(turn_of, side):
        return pltpu.make_async_remote_copy(
            src_ref=out_face.at[turn_of, side],
            dst_ref=in_face.at[turn_of, side],
            send_sem=face_send.at[turn_of, side],
            recv_sem=face_recv.at[turn_of, side],
            device_id=sides[side][2],
            device_id_type=pl.DeviceIdType.MESH,
        )

    def exchange_start(turn_of, x):
        x0, x1, y0, y1 = faces(x)
        last = jnp.where(live == 1, x1, jnp.where(live == 2, roll(x1, -2, 0), jnp.where(live == 3, roll(x1, -4, 0), roll(x1, -6, 0))))
        out_face[turn_of, 0] = last
        out_face[turn_of, 1] = x0
        out_face[turn_of, 2] = y1
        out_face[turn_of, 3] = y0
        for side in range(4):
            @pl.when(sides[side][0])
            def _():
                face_copy(turn_of, side).start()
        return x0, x1

    def exchange_end(turn_of, x0, x1):
        for side in range(4):
            @pl.when(sides[side][1])
            def _():
                face_copy(turn_of, side).wait_recv()
        right = keep(row8 < 2, in_face[turn_of, 1])
        right = right + roll(right, 2, 0)
        right = right + roll(right, 4, 0)
        gx0 = jnp.where(row8 < 2, in_face[turn_of, 0], roll(x1, 2, 0))
        gx1 = jnp.where(row8 < 2 * (live - 1), roll(x0, -2, 0), right)
        gy0 = in_face[turn_of, 2]
        gy1 = in_face[turn_of, 3]
        flipped = flip(jnp.concatenate([gx0, gx1, gy0, gy1], 0))
        fx0, fx1, fy0, fy1 = flipped[:8], flipped[8:16], flipped[16:24], flipped[24:]
        gu0 = pick(turn, gx0, fy0, fx1, gy1)
        gu1 = pick(turn, gx1, fy1, fx0, gy0)
        gv0 = pick(turn, gy0, gx1, fy1, fx0)
        gv1 = pick(turn, gy1, gx0, fy0, fx1)
        lo = jnp.where(u64 == 0, unfold(gu0), keep(u64 == 15, unfold(roll(gu1, 1, 0))))
        hi = jnp.where(u64 == 0, unfold(roll(gu0, -1, 0)), keep(u64 == 15, unfold(gu1)))
        rim_u = jnp.concatenate([lo, hi], 0)
        lo = keep(grid.g == 0, spread(keep(diagonal_face, unfold(gv0))))
        hi = keep(grid.g == 7, spread(keep(diagonal_face, unfold(gv1))))
        rim_v = jnp.concatenate([lo, hi], 0)
        return rim_u, rim_v

    def operate(x, rim_u, rim_v):
        return keep(alive, (6.0 + coef) * x - (grid.near(x, 1) + (rim_u + rim_v)))

    def inner(a, b):
        return (a * b).reshape(16, 8, 128).sum(0)

    z0 = vcycle(grid, r0, inverse, 0)
    pl.semaphore_wait(barrier, n_slab - 1 + n_cross - 1)
    z_faces = exchange_start(0, z0)
    dot_rz = inner(r0, z0)
    z_rims = exchange_end(0, *z_faces)
    q0 = operate(z0, *z_rims)
    w0 = vcycle(grid, q0, inverse, 0)
    w_faces = exchange_start(1, w0)
    dot_zq = inner(z0, q0)
    dot_rw = inner(r0, w0)
    dot_qw = inner(q0, w0)
    w_rims = exchange_end(1, *w_faces)
    dot_wv = inner(w0, operate(w0, *w_rims))
    none = jnp.zeros((8, 128), jnp.float32)
    partial = jnp.concatenate([dot_rz, dot_zq, dot_rw, dot_qw, dot_wv, none, none, none], 0)
    partial = partial.reshape(8, 8, 128).sum(1)

    def total(value, own, count, me, out, into, send, recv, place):
        out[...] = value

        def copy(source, target):
            return pltpu.make_async_remote_copy(
                src_ref=out, dst_ref=into.at[source], send_sem=send.at[target], recv_sem=recv.at[source],
                device_id=place(target), device_id_type=pl.DeviceIdType.MESH,
            )

        def begin(step):
            copy(me, lax.rem(me + step, count)).start()

        def arrive(step):
            copy(lax.rem(me + step, count), lax.rem(me + step, count)).wait_recv()

        def leave(step):
            copy(me, lax.rem(me + step, count)).wait_send()

        each(count, begin)
        into[me] = value
        each(count, arrive)
        result = into[...].sum(0)
        return result, lambda: each(count, leave)

    across, leave_slab = total(partial, slab, n_slab, slab, mine, sums, sum_send, sum_recv, lambda k: (k, cross))
    whole, leave_cross = total(across, cross, n_cross, cross, mine_z, sums_z, sum_send_z, sum_recv_z, lambda k: (slab, k))
    whole = jnp.sum(whole, 1, keepdims=True)
    rz, zq, rw, qw, wv = (whole[k : k + 1] for k in range(5))
    alpha = rz / zq
    rz_new = rz - alpha * (zq + rw) + alpha * alpha * qw
    gain = 1.0 + rz_new / rz
    pq = gain * gain * zq - 2.0 * gain * alpha * qw + alpha * alpha * wv
    step = rz_new / pq
    of_z = alpha + step * gain
    of_w = -step * alpha
    x = of_z * z0 + of_w * w0
    rim_u = of_z * z_rims[0] + of_w * w_rims[0]
    rim_v = of_z * z_rims[1] + of_w * w_rims[1]
    prev_u, next_u, prev_v, next_v, prev_w, next_w = grid.shifts(x, 1)
    rim_u = jnp.where(grid.u == 0, -rim_u, rim_u)
    rim_v = jnp.concatenate([-rim_v[:64], rim_v[64:]], 0)

    def store(ref, value):
        ref[...] = jnp.concatenate([value[:64], value[64:]], 1)

    store(pot_ref, x)
    store(vel_ref.at[0], keep(alive, 0.5 * (next_u - prev_u + rim_u)))
    store(vel_ref.at[1], keep(alive, 0.5 * (next_v - prev_v + rim_v)))
    store(vel_ref.at[2], keep(alive, 0.5 * (next_w - prev_w)))

    leave_slab()
    leave_cross()
    for turn_of in range(2):
        for side in range(4):
            @pl.when(sides[side][0])
            def _():
                face_copy(turn_of, side).wait_send()


def local(n_slab, n_cross, source, reaction, counts, orientation):
    slots, length = source.shape[1], source.shape[3]
    rows, lanes = slots * length, length * length
    dma = pltpu.SemaphoreType.DMA
    vmem = pl.BlockSpec(memory_space=pltpu.VMEM)
    hbm = pl.BlockSpec(memory_space=pltpu.HBM)
    potential, velocity = pl.pallas_call(
        functools.partial(kernel, n_slab, n_cross),
        out_shape=(
            jax.ShapeDtypeStruct((rows, lanes), jnp.float32),
            jax.ShapeDtypeStruct((3, rows, lanes), jnp.float32),
        ),
        in_specs=[hbm, hbm, hbm, hbm],
        out_specs=(vmem, vmem),
        scratch_shapes=[
            pltpu.SMEM(counts.shape, jnp.int32),
            pltpu.SMEM((slots,), jnp.int32),
            pltpu.VMEM((rows, lanes), jnp.float32),
            pltpu.VMEM((rows, lanes), jnp.float32),
            dma((4,)),
            pltpu.VMEM((2, 4, 8, 128), jnp.float32),
            pltpu.VMEM((2, 4, 8, 128), jnp.float32),
            dma((2, 4)),
            dma((2, 4)),
            pltpu.VMEM((8, 128), jnp.float32),
            pltpu.VMEM((n_slab, 8, 128), jnp.float32),
            dma((n_slab,)),
            dma((n_slab,)),
            pltpu.VMEM((8, 128), jnp.float32),
            pltpu.VMEM((n_cross, 8, 128), jnp.float32),
            dma((n_cross,)),
            dma((n_cross,)),
        ],
        compiler_params=pltpu.CompilerParams(
            collective_id=0, has_side_effects=True, vmem_limit_bytes=56 * 2**20
        ),
    )(counts, orientation.reshape(slots), source.reshape(rows, lanes), reaction.reshape(rows, lanes))
    return potential.reshape(source.shape), velocity.reshape((3,) + source.shape)


def solution(mesh):
    spec = P("slab", None, "cross", None, None)
    return jax.shard_map(
        functools.partial(local, mesh.shape["slab"], mesh.shape["cross"]),
        mesh=mesh,
        in_specs=(spec, spec, P(), P("slab", None, "cross")),
        out_specs=(spec, P(None, "slab", None, "cross", None, None)),
        check_vma=False,
    )
```

```python
import functools

import jax
import jax.numpy as jnp
from jax import lax
from jax.experimental import pallas as pl
from jax.experimental.pallas import tpu as pltpu
from jax.sharding import PartitionSpec as P

LEVELS = 4
SWEEPS = 4
DAMPING = 0.8
KEEP = 1.0 - DAMPING


def roll(x, shift, axis):
    return pltpu.roll(x, shift % x.shape[axis], axis)


def iota(shape, axis):
    return lax.broadcasted_iota(jnp.int32, shape, axis)


def keep(mask, x):
    return jnp.where(mask, x, 0.0)


class Grid:
    def __init__(self):
        self.u = iota((128, 128), 0) % 16
        self.w = iota((128, 128), 1) % 16
        self.g = iota((64, 128), 1) // 16
        self.gg = iota((128, 128), 1) // 16

    def shifts(self, x, d):
        prev_u = keep(self.u >= d, roll(x, d, 0))
        next_u = keep(self.u < 16 - d, roll(x, -d, 0))
        prev_w = keep(self.w >= d, roll(x, d, 1))
        next_w = keep(self.w < 16 - d, roll(x, -d, 1))
        up = roll(x, 16 * d, 1)
        down = roll(x, -16 * d, 1)
        inside = self.g >= d
        prev_v = jnp.concatenate([keep(inside, up[:64]), jnp.where(inside, up[64:], up[:64])], 0)
        inside = self.g < 8 - d
        next_v = jnp.concatenate([jnp.where(inside, down[:64], down[64:]), keep(inside, down[64:])], 0)
        return prev_u, next_u, prev_v, next_v, prev_w, next_w

    def near(self, x, d):
        if d == 8:
            swap_u = x.reshape(8, 2, 8, 128)
            swap_u = jnp.concatenate([swap_u[:, 1:], swap_u[:, :1]], 1).reshape(128, 128)
            swap_v = jnp.concatenate([x[64:], x[:64]], 0)
            swap_w = jnp.where(self.w >= 8, roll(x, 8, 1), roll(x, -8, 1))
            return swap_u + swap_v + swap_w
        prev_u, next_u, prev_v, next_v, prev_w, next_w = self.shifts(x, d)
        return (prev_u + next_u) + (prev_v + next_v) + (prev_w + next_w)

    def restrict(self, x, d):
        x = x + jnp.where((self.u & d) != 0, roll(x, d, 0), roll(x, -d, 0))
        if d == 4:
            x = x + roll(x, 64, 1)
        else:
            x = x + jnp.where((self.gg & d) != 0, roll(x, 16 * d, 1), roll(x, -16 * d, 1))
        x = x + jnp.where((self.w & d) != 0, roll(x, d, 1), roll(x, -d, 1))
        return x * 0.125


def vcycle(grid, f, inverse, level):
    d = 2**level
    scale = 4.0**-level
    inv = inverse[level]
    e = inv * f
    if level == LEVELS - 1:
        for _ in range(SWEEPS - 1):
            e = KEEP * e + inv * (f + scale * grid.near(e, d))
        return e
    e = e + vcycle(grid, grid.restrict(KEEP * f + scale * grid.near(e, d), d), inverse, level + 1)
    return KEEP * e + inv * (f + scale * grid.near(e, d))


def fold(x):
    return x.reshape(8, 8, 128).sum(1)


def unfold(x):
    return jnp.broadcast_to(x[:, None, :], (8, 8, 128)).reshape(64, 128)


def spread(x):
    x = x + roll(x, 16, 1)
    x = x + roll(x, 32, 1)
    return x + roll(x, 64, 1)


def flip(x):
    row = iota(x.shape, 0)
    group = iota(x.shape, 1) // 16
    x = jnp.where(row % 2 == 1, roll(x, 1, 0), roll(x, -1, 0))
    x = roll(x, 64, 1)
    x = jnp.where((group & 2) != 0, roll(x, 32, 1), roll(x, -32, 1))
    return jnp.where((group & 1) != 0, roll(x, 16, 1), roll(x, -16, 1))


def pick(turn, a, b, c, d):
    return jnp.where(turn == 0, a, jnp.where(turn == 1, b, jnp.where(turn == 2, c, d)))


def kernel(
    n_slab, n_cross, counts_hbm, turn_hbm, source_hbm, reaction_hbm, pot_ref, vel_ref,
    counts_ref, turn_ref, source_ref, reaction_ref, load_sem,
    out_face, in_face, face_send, face_recv, mine, sums, sum_send, sum_recv,
    mine_z, sums_z, sum_send_z, sum_recv_z,
):
    slab = lax.axis_index("slab")
    cross = lax.axis_index("cross")

    loads = []
    pairs = ((counts_hbm, counts_ref), (reaction_hbm, reaction_ref), (turn_hbm, turn_ref), (source_hbm, source_ref))
    for place, (there, here) in enumerate(pairs):
        loads.append(pltpu.make_async_copy(there, here, load_sem.at[place]))
        loads[-1].start()

    in_face[...] = jnp.zeros_like(in_face)
    barrier = pltpu.get_barrier_semaphore()

    def each(count, body):
        if count <= 32:
            for step in range(1, count):
                body(step)
        else:
            lax.fori_loop(1, count, lambda step, carry: (body(step), carry)[1], 0)

    def greet_slab(step):
        pl.semaphore_signal(barrier, inc=1, device_id=(lax.rem(slab + step, n_slab), cross), device_id_type=pl.DeviceIdType.MESH)

    def greet_cross(step):
        pl.semaphore_signal(barrier, inc=1, device_id=(slab, lax.rem(cross + step, n_cross)), device_id_type=pl.DeviceIdType.MESH)

    devices = n_slab * n_cross
    direct = devices <= 64
    me = slab * n_cross + cross

    def seat(k):
        return k // n_cross, lax.rem(k, n_cross)

    def greet(step):
        pl.semaphore_signal(barrier, inc=1, device_id=seat(lax.rem(me + step, devices)), device_id_type=pl.DeviceIdType.MESH)

    if direct:
        each(devices, greet)
    else:
        each(n_slab, greet_slab)
        each(n_cross, greet_cross)

    grid = Grid()
    for each_load in loads:
        each_load.wait()
    live = counts_ref[slab]
    row8 = iota((8, 128), 0)
    turn = jnp.where(row8 < 2, turn_ref[0], jnp.where(row8 < 4, turn_ref[1], jnp.where(row8 < 6, turn_ref[2], turn_ref[3])))
    alive = (iota((128, 128), 0) % 64) // 16 < live
    u64 = grid.u[:64]
    diagonal_face = u64 % 8 == grid.g

    def load(ref):
        x = ref[...]
        return jnp.concatenate([x[:, :128], x[:, 128:]], 0)

    r0 = keep(alive, load(source_ref))
    coef = jnp.where(alive, load(reaction_ref), 1.0)
    inverse = []
    level_coef = coef
    for level in range(LEVELS):
        inverse.append(DAMPING / (6.0 * 4.0**-level + level_coef))
        if level + 1 < LEVELS:
            level_coef = grid.restrict(level_coef, 2**level)

    def faces(x):
        lo, hi = x[:64], x[64:]
        u0 = fold(keep(u64 == 0, lo)) + roll(fold(keep(u64 == 0, hi)), 1, 0)
        u1 = roll(fold(keep(u64 == 15, lo)), -1, 0) + fold(keep(u64 == 15, hi))
        v0 = fold(keep(diagonal_face, spread(keep(grid.g == 0, lo))))
        v1 = fold(keep(diagonal_face, spread(keep(grid.g == 7, hi))))
        flipped = flip(jnp.concatenate([u0, u1, v0, v1], 0))
        fu0, fu1, fv0, fv1 = flipped[:8], flipped[8:16], flipped[16:24], flipped[24:]
        return (
            pick(turn, u0, v1, fu1, fv0),
            pick(turn, u1, v0, fu0, fv1),
            pick(turn, v0, fu0, fv1, u1),
            pick(turn, v1, fu1, fv0, u0),
        )

    sides = (
        (slab + 1 < n_slab, slab > 0, (slab + 1, cross)),
        (slab > 0, slab + 1 < n_slab, (slab - 1, cross)),
        (cross + 1 < n_cross, cross > 0, (slab, cross + 1)),
        (cross > 0, cross + 1 < n_cross, (slab, cross - 1)),
    )

    def face_copy(turn_of, side):
        return pltpu.make_async_remote_copy(
            src_ref=out_face.at[turn_of, side],
            dst_ref=in_face.at[turn_of, side],
            send_sem=face_send.at[turn_of, side],
            recv_sem=face_recv.at[turn_of, side],
            device_id=sides[side][2],
            device_id_type=pl.DeviceIdType.MESH,
        )

    def exchange_start(turn_of, x):
        x0, x1, y0, y1 = faces(x)
        last = jnp.where(live == 1, x1, jnp.where(live == 2, roll(x1, -2, 0), jnp.where(live == 3, roll(x1, -4, 0), roll(x1, -6, 0))))
        out_face[turn_of, 0] = last
        out_face[turn_of, 1] = x0
        out_face[turn_of, 2] = y1
        out_face[turn_of, 3] = y0
        for side in range(4):
            @pl.when(sides[side][0])
            def _():
                face_copy(turn_of, side).start()
        return x0, x1

    def exchange_end(turn_of, x0, x1):
        for side in range(4):
            @pl.when(sides[side][1])
            def _():
                face_copy(turn_of, side).wait_recv()
        right = keep(row8 < 2, in_face[turn_of, 1])
        right = right + roll(right, 2, 0)
        right = right + roll(right, 4, 0)
        gx0 = jnp.where(row8 < 2, in_face[turn_of, 0], roll(x1, 2, 0))
        gx1 = jnp.where(row8 < 2 * (live - 1), roll(x0, -2, 0), right)
        gy0 = in_face[turn_of, 2]
        gy1 = in_face[turn_of, 3]
        flipped = flip(jnp.concatenate([gx0, gx1, gy0, gy1], 0))
        fx0, fx1, fy0, fy1 = flipped[:8], flipped[8:16], flipped[16:24], flipped[24:]
        gu0 = pick(turn, gx0, fy0, fx1, gy1)
        gu1 = pick(turn, gx1, fy1, fx0, gy0)
        gv0 = pick(turn, gy0, gx1, fy1, fx0)
        gv1 = pick(turn, gy1, gx0, fy0, fx1)
        lo = jnp.where(u64 == 0, unfold(gu0), keep(u64 == 15, unfold(roll(gu1, 1, 0))))
        hi = jnp.where(u64 == 0, unfold(roll(gu0, -1, 0)), keep(u64 == 15, unfold(gu1)))
        rim_u = jnp.concatenate([lo, hi], 0)
        lo = keep(grid.g == 0, spread(keep(diagonal_face, unfold(gv0))))
        hi = keep(grid.g == 7, spread(keep(diagonal_face, unfold(gv1))))
        rim_v = jnp.concatenate([lo, hi], 0)
        return rim_u, rim_v

    def operate(x, rim_u, rim_v):
        return keep(alive, (6.0 + coef) * x - (grid.near(x, 1) + (rim_u + rim_v)))

    def inner(a, b):
        return (a * b).reshape(16, 8, 128).sum(0)

    z0 = vcycle(grid, r0, inverse, 0)
    pl.semaphore_wait(barrier, devices - 1 if direct else n_slab - 1 + n_cross - 1)
    z_faces = exchange_start(0, z0)
    dot_rz = inner(r0, z0)
    z_rims = exchange_end(0, *z_faces)
    q0 = operate(z0, *z_rims)
    w0 = vcycle(grid, q0, inverse, 0)
    w_faces = exchange_start(1, w0)
    dot_zq = inner(z0, q0)
    dot_rw = inner(r0, w0)
    dot_qw = inner(q0, w0)
    w_rims = exchange_end(1, *w_faces)
    dot_wv = inner(w0, operate(w0, *w_rims))
    none = jnp.zeros((8, 128), jnp.float32)
    partial = jnp.concatenate([dot_rz, dot_zq, dot_rw, dot_qw, dot_wv, none, none, none], 0)
    partial = partial.reshape(8, 8, 128).sum(1)

    def total(value, count, me, out, into, send, recv, place):
        out[...] = value

        def copy(source, target):
            return pltpu.make_async_remote_copy(
                src_ref=out, dst_ref=into.at[source], send_sem=send.at[target], recv_sem=recv.at[source],
                device_id=place(target), device_id_type=pl.DeviceIdType.MESH,
            )

        def begin(step):
            copy(me, lax.rem(me + step, count)).start()

        def arrive(step):
            copy(lax.rem(me + step, count), lax.rem(me + step, count)).wait_recv()

        def leave(step):
            copy(me, lax.rem(me + step, count)).wait_send()

        each(count, begin)
        into[me] = value
        each(count, arrive)
        result = into[...].sum(0)
        return result, lambda: each(count, leave)

    if direct:
        whole, leave = total(partial, devices, me, mine, sums, sum_send, sum_recv, seat)
        leaves = (leave,)
    else:
        across, leave_slab = total(partial, n_slab, slab, mine, sums, sum_send, sum_recv, lambda k: (k, cross))
        whole, leave_cross = total(across, n_cross, cross, mine_z, sums_z, sum_send_z, sum_recv_z, lambda k: (slab, k))
        leaves = (leave_slab, leave_cross)
    whole = jnp.sum(whole, 1, keepdims=True)
    rz, zq, rw, qw, wv = (whole[k : k + 1] for k in range(5))
    alpha = rz / zq
    rz_new = rz - alpha * (zq + rw) + alpha * alpha * qw
    gain = 1.0 + rz_new / rz
    pq = gain * gain * zq - 2.0 * gain * alpha * qw + alpha * alpha * wv
    step = rz_new / pq
    of_z = alpha + step * gain
    of_w = -step * alpha
    x = of_z * z0 + of_w * w0
    rim_u = of_z * z_rims[0] + of_w * w_rims[0]
    rim_v = of_z * z_rims[1] + of_w * w_rims[1]
    prev_u, next_u, prev_v, next_v, prev_w, next_w = grid.shifts(x, 1)
    rim_u = jnp.where(grid.u == 0, -rim_u, rim_u)
    rim_v = jnp.concatenate([-rim_v[:64], rim_v[64:]], 0)

    def store(ref, value):
        ref[...] = jnp.concatenate([value[:64], value[64:]], 1)

    store(pot_ref, x)
    store(vel_ref.at[0], keep(alive, 0.5 * (next_u - prev_u + rim_u)))
    store(vel_ref.at[1], keep(alive, 0.5 * (next_v - prev_v + rim_v)))
    store(vel_ref.at[2], keep(alive, 0.5 * (next_w - prev_w)))

    for leave in leaves:
        leave()
    for turn_of in range(2):
        for side in range(4):
            @pl.when(sides[side][0])
            def _():
                face_copy(turn_of, side).wait_send()


def local(n_slab, n_cross, source, reaction, counts, orientation):
    slots, length = source.shape[1], source.shape[3]
    rows, lanes = slots * length, length * length
    first = n_slab * n_cross if n_slab * n_cross <= 64 else n_slab
    dma = pltpu.SemaphoreType.DMA
    vmem = pl.BlockSpec(memory_space=pltpu.VMEM)
    hbm = pl.BlockSpec(memory_space=pltpu.HBM)
    potential, velocity = pl.pallas_call(
        functools.partial(kernel, n_slab, n_cross),
        out_shape=(
            jax.ShapeDtypeStruct((rows, lanes), jnp.float32),
            jax.ShapeDtypeStruct((3, rows, lanes), jnp.float32),
        ),
        in_specs=[hbm, hbm, hbm, hbm],
        out_specs=(vmem, vmem),
        scratch_shapes=[
            pltpu.SMEM(counts.shape, jnp.int32),
            pltpu.SMEM((slots,), jnp.int32),
            pltpu.VMEM((rows, lanes), jnp.float32),
            pltpu.VMEM((rows, lanes), jnp.float32),
            dma((4,)),
            pltpu.VMEM((2, 4, 8, 128), jnp.float32),
            pltpu.VMEM((2, 4, 8, 128), jnp.float32),
            dma((2, 4)),
            dma((2, 4)),
            pltpu.VMEM((8, 128), jnp.float32),
            pltpu.VMEM((first, 8, 128), jnp.float32),
            dma((first,)),
            dma((first,)),
            pltpu.VMEM((8, 128), jnp.float32),
            pltpu.VMEM((n_cross, 8, 128), jnp.float32),
            dma((n_cross,)),
            dma((n_cross,)),
        ],
        compiler_params=pltpu.CompilerParams(
            collective_id=0, has_side_effects=True, vmem_limit_bytes=16 * 2**20
        ),
    )(
        *(
            pltpu.with_memory_space_constraint(x, pltpu.HBM)
            for x in (counts, orientation.reshape(slots), source.reshape(rows, lanes), reaction.reshape(rows, lanes))
        )
    )
    return potential.reshape(source.shape), velocity.reshape((3,) + source.shape)


def solution(mesh):
    spec = P("slab", None, "cross", None, None)
    return jax.shard_map(
        functools.partial(local, mesh.shape["slab"], mesh.shape["cross"]),
        mesh=mesh,
        in_specs=(spec, spec, P(), P("slab", None, "cross")),
        out_specs=(spec, P(None, "slab", None, "cross", None, None)),
        check_vma=False,
    )
```

```python
import functools

import jax
import jax.numpy as jnp
from jax import lax
from jax.experimental import pallas as pl
from jax.experimental.pallas import tpu as pltpu
from jax.sharding import PartitionSpec as P

LEVELS = 4
SWEEPS = 4
DAMPING = 0.8
KEEP = 1.0 - DAMPING


def roll(x, shift, axis):
    return pltpu.roll(x, shift % x.shape[axis], axis)


def iota(shape, axis):
    return lax.broadcasted_iota(jnp.int32, shape, axis)


def keep(mask, x):
    return jnp.where(mask, x, 0.0)


class Grid:
    def __init__(self):
        self.u = iota((128, 128), 0) % 16
        self.w = iota((128, 128), 1) % 16
        self.g = iota((64, 128), 1) // 16
        self.gg = iota((128, 128), 1) // 16

    def shifts(self, x, d):
        prev_u = keep(self.u >= d, roll(x, d, 0))
        next_u = keep(self.u < 16 - d, roll(x, -d, 0))
        prev_w = keep(self.w >= d, roll(x, d, 1))
        next_w = keep(self.w < 16 - d, roll(x, -d, 1))
        up = roll(x, 16 * d, 1)
        down = roll(x, -16 * d, 1)
        inside = self.g >= d
        prev_v = jnp.concatenate([keep(inside, up[:64]), jnp.where(inside, up[64:], up[:64])], 0)
        inside = self.g < 8 - d
        next_v = jnp.concatenate([jnp.where(inside, down[:64], down[64:]), keep(inside, down[64:])], 0)
        return prev_u, next_u, prev_v, next_v, prev_w, next_w

    def near(self, x, d):
        if d == 8:
            swap_u = x.reshape(8, 2, 8, 128)
            swap_u = jnp.concatenate([swap_u[:, 1:], swap_u[:, :1]], 1).reshape(128, 128)
            swap_v = jnp.concatenate([x[64:], x[:64]], 0)
            swap_w = jnp.where(self.w >= 8, roll(x, 8, 1), roll(x, -8, 1))
            return swap_u + swap_v + swap_w
        prev_u, next_u, prev_v, next_v, prev_w, next_w = self.shifts(x, d)
        return (prev_u + next_u) + (prev_v + next_v) + (prev_w + next_w)

    def restrict(self, x, d):
        x = x + jnp.where((self.u & d) != 0, roll(x, d, 0), roll(x, -d, 0))
        if d == 4:
            x = x + roll(x, 64, 1)
        else:
            x = x + jnp.where((self.gg & d) != 0, roll(x, 16 * d, 1), roll(x, -16 * d, 1))
        x = x + jnp.where((self.w & d) != 0, roll(x, d, 1), roll(x, -d, 1))
        return x * 0.125


def vcycle(grid, f, inverse, level):
    d = 2**level
    scale = 4.0**-level
    inv = inverse[level]
    e = inv * f
    if level == LEVELS - 1:
        for _ in range(SWEEPS - 1):
            e = KEEP * e + inv * (f + scale * grid.near(e, d))
        return e
    e = e + vcycle(grid, grid.restrict(KEEP * f + scale * grid.near(e, d), d), inverse, level + 1)
    return KEEP * e + inv * (f + scale * grid.near(e, d))


def fold(x):
    return x.reshape(8, 8, 128).sum(1)


def unfold(x):
    return jnp.broadcast_to(x[:, None, :], (8, 8, 128)).reshape(64, 128)


def spread(x):
    x = x + roll(x, 16, 1)
    x = x + roll(x, 32, 1)
    return x + roll(x, 64, 1)


def flip(x):
    row = iota(x.shape, 0)
    group = iota(x.shape, 1) // 16
    x = jnp.where(row % 2 == 1, roll(x, 1, 0), roll(x, -1, 0))
    x = roll(x, 64, 1)
    x = jnp.where((group & 2) != 0, roll(x, 32, 1), roll(x, -32, 1))
    return jnp.where((group & 1) != 0, roll(x, 16, 1), roll(x, -16, 1))


def pick(turn, a, b, c, d):
    return jnp.where(turn == 0, a, jnp.where(turn == 1, b, jnp.where(turn == 2, c, d)))


def kernel(
    n_slab, n_cross, counts_hbm, turn_hbm, source_hbm, reaction_hbm, pot_ref, vel_ref,
    counts_ref, turn_ref, source_ref, reaction_ref, load_sem,
    out_face, in_face, face_send, face_recv, mine, sums, sum_send, sum_recv,
    mine_z, sums_z, sum_send_z, sum_recv_z,
):
    slab = lax.axis_index("slab")
    cross = lax.axis_index("cross")

    loads = []
    pairs = ((counts_hbm, counts_ref), (reaction_hbm, reaction_ref), (turn_hbm, turn_ref), (source_hbm, source_ref))
    for place, (there, here) in enumerate(pairs):
        loads.append(pltpu.make_async_copy(there, here, load_sem.at[place]))
        loads[-1].start()

    in_face[...] = jnp.zeros_like(in_face)
    barrier = pltpu.get_barrier_semaphore()

    def each(count, body):
        if count <= 32:
            for step in range(1, count):
                body(step)
        else:
            lax.fori_loop(1, count, lambda step, carry: (body(step), carry)[1], 0)

    def greet_slab(step):
        pl.semaphore_signal(barrier, inc=1, device_id=(lax.rem(slab + step, n_slab), cross), device_id_type=pl.DeviceIdType.MESH)

    def greet_cross(step):
        pl.semaphore_signal(barrier, inc=1, device_id=(slab, lax.rem(cross + step, n_cross)), device_id_type=pl.DeviceIdType.MESH)

    devices = n_slab * n_cross
    direct = devices <= 64
    me = slab * n_cross + cross

    def seat(k):
        return k // n_cross, lax.rem(k, n_cross)

    def greet(step):
        pl.semaphore_signal(barrier, inc=1, device_id=seat(lax.rem(me + step, devices)), device_id_type=pl.DeviceIdType.MESH)

    if direct:
        each(devices, greet)
    else:
        each(n_slab, greet_slab)
        each(n_cross, greet_cross)

    grid = Grid()
    for each_load in loads:
        each_load.wait()
    live = counts_ref[slab]
    row8 = iota((8, 128), 0)
    turn = jnp.where(row8 < 2, turn_ref[0], jnp.where(row8 < 4, turn_ref[1], jnp.where(row8 < 6, turn_ref[2], turn_ref[3])))
    alive = (iota((128, 128), 0) % 64) // 16 < live
    u64 = grid.u[:64]
    diagonal_face = u64 % 8 == grid.g

    def load(ref):
        x = ref[...]
        return jnp.concatenate([x[:, :128], x[:, 128:]], 0)

    r0 = keep(alive, load(source_ref))
    coef = jnp.where(alive, load(reaction_ref), 1.0)
    inverse = []
    level_coef = coef
    for level in range(LEVELS):
        inverse.append(DAMPING / (6.0 * 4.0**-level + level_coef))
        if level + 1 < LEVELS:
            level_coef = grid.restrict(level_coef, 2**level)

    def faces(x):
        lo, hi = x[:64], x[64:]
        u0 = fold(keep(u64 == 0, lo)) + roll(fold(keep(u64 == 0, hi)), 1, 0)
        u1 = roll(fold(keep(u64 == 15, lo)), -1, 0) + fold(keep(u64 == 15, hi))
        v0 = fold(keep(diagonal_face, spread(keep(grid.g == 0, lo))))
        v1 = fold(keep(diagonal_face, spread(keep(grid.g == 7, hi))))
        flipped = flip(jnp.concatenate([u0, u1, v0, v1], 0))
        fu0, fu1, fv0, fv1 = flipped[:8], flipped[8:16], flipped[16:24], flipped[24:]
        return (
            pick(turn, u0, v1, fu1, fv0),
            pick(turn, u1, v0, fu0, fv1),
            pick(turn, v0, fu0, fv1, u1),
            pick(turn, v1, fu1, fv0, u0),
        )

    sides = (
        (slab + 1 < n_slab, slab > 0, (slab + 1, cross)),
        (slab > 0, slab + 1 < n_slab, (slab - 1, cross)),
        (cross + 1 < n_cross, cross > 0, (slab, cross + 1)),
        (cross > 0, cross + 1 < n_cross, (slab, cross - 1)),
    )

    def face_copy(turn_of, side):
        return pltpu.make_async_remote_copy(
            src_ref=out_face.at[turn_of, side],
            dst_ref=in_face.at[turn_of, side],
            send_sem=face_send.at[turn_of, side],
            recv_sem=face_recv.at[turn_of, side],
            device_id=sides[side][2],
            device_id_type=pl.DeviceIdType.MESH,
        )

    def exchange_start(turn_of, x):
        x0, x1, y0, y1 = faces(x)
        last = jnp.where(live == 1, x1, jnp.where(live == 2, roll(x1, -2, 0), jnp.where(live == 3, roll(x1, -4, 0), roll(x1, -6, 0))))
        out_face[turn_of, 0] = last
        out_face[turn_of, 1] = x0
        out_face[turn_of, 2] = y1
        out_face[turn_of, 3] = y0
        for side in range(4):
            @pl.when(sides[side][0])
            def _():
                face_copy(turn_of, side).start()
        return x0, x1

    def exchange_end(turn_of, x0, x1):
        for side in range(4):
            @pl.when(sides[side][1])
            def _():
                face_copy(turn_of, side).wait_recv()
        right = keep(row8 < 2, in_face[turn_of, 1])
        right = right + roll(right, 2, 0)
        right = right + roll(right, 4, 0)
        gx0 = jnp.where(row8 < 2, in_face[turn_of, 0], roll(x1, 2, 0))
        gx1 = jnp.where(row8 < 2 * (live - 1), roll(x0, -2, 0), right)
        gy0 = in_face[turn_of, 2]
        gy1 = in_face[turn_of, 3]
        flipped = flip(jnp.concatenate([gx0, gx1, gy0, gy1], 0))
        fx0, fx1, fy0, fy1 = flipped[:8], flipped[8:16], flipped[16:24], flipped[24:]
        gu0 = pick(turn, gx0, fy0, fx1, gy1)
        gu1 = pick(turn, gx1, fy1, fx0, gy0)
        gv0 = pick(turn, gy0, gx1, fy1, fx0)
        gv1 = pick(turn, gy1, gx0, fy0, fx1)
        lo = jnp.where(u64 == 0, unfold(gu0), keep(u64 == 15, unfold(roll(gu1, 1, 0))))
        hi = jnp.where(u64 == 0, unfold(roll(gu0, -1, 0)), keep(u64 == 15, unfold(gu1)))
        rim_u = jnp.concatenate([lo, hi], 0)
        lo = keep(grid.g == 0, spread(keep(diagonal_face, unfold(gv0))))
        hi = keep(grid.g == 7, spread(keep(diagonal_face, unfold(gv1))))
        rim_v = jnp.concatenate([lo, hi], 0)
        return rim_u, rim_v

    def interior(x):
        prev_u, next_u, prev_v, next_v, prev_w, next_w = grid.shifts(x, 1)
        image = (6.0 + coef) * x - ((prev_u + next_u) + (prev_v + next_v) + (prev_w + next_w))
        return image, next_u - prev_u, next_v - prev_v, keep(alive, 0.5 * (next_w - prev_w))

    def gradient(inside, rim_u, rim_v):
        along_u = inside[1] + jnp.where(grid.u == 0, -rim_u, rim_u)
        along_v = inside[2] + jnp.concatenate([-rim_v[:64], rim_v[64:]], 0)
        return keep(alive, 0.5 * along_u), keep(alive, 0.5 * along_v), inside[3]

    def inner(a, b):
        return (a * b).reshape(16, 8, 128).sum(0)

    z0 = vcycle(grid, r0, inverse, 0)
    pl.semaphore_wait(barrier, devices - 1 if direct else n_slab - 1 + n_cross - 1)
    z_faces = exchange_start(0, z0)
    dot_rz = inner(r0, z0)
    z_inside = interior(z0)
    z_rims = exchange_end(0, *z_faces)
    q0 = keep(alive, z_inside[0] - (z_rims[0] + z_rims[1]))
    w0 = vcycle(grid, q0, inverse, 0)
    w_faces = exchange_start(1, w0)
    dot_zq = inner(z0, q0)
    dot_rw = inner(r0, w0)
    dot_qw = inner(q0, w0)
    w_inside = interior(w0)
    w_rims = exchange_end(1, *w_faces)
    dot_wv = inner(w0, w_inside[0] - (w_rims[0] + w_rims[1]))
    none = jnp.zeros((8, 128), jnp.float32)
    partial = jnp.concatenate([dot_rz, dot_zq, dot_rw, dot_qw, dot_wv, none, none, none], 0)
    partial = partial.reshape(8, 8, 128).sum(1)

    def total(value, count, me, out, into, send, recv, place, beside):
        out[...] = value

        def copy(source, target):
            return pltpu.make_async_remote_copy(
                src_ref=out, dst_ref=into.at[source], send_sem=send.at[target], recv_sem=recv.at[source],
                device_id=place(target), device_id_type=pl.DeviceIdType.MESH,
            )

        def begin(step):
            copy(me, lax.rem(me + step, count)).start()

        def arrive(step):
            copy(lax.rem(me + step, count), lax.rem(me + step, count)).wait_recv()

        def leave(step):
            copy(me, lax.rem(me + step, count)).wait_send()

        each(count, begin)
        meanwhile = beside()
        into[me] = value
        each(count, arrive)
        result = into[...].sum(0)
        return result, meanwhile, lambda: each(count, leave)

    def gradients():
        return gradient(z_inside, *z_rims), gradient(w_inside, *w_rims)

    if direct:
        whole, slopes, leave = total(partial, devices, me, mine, sums, sum_send, sum_recv, seat, gradients)
        leaves = (leave,)
    else:
        across, slopes, leave_slab = total(partial, n_slab, slab, mine, sums, sum_send, sum_recv, lambda k: (k, cross), gradients)
        whole, _, leave_cross = total(across, n_cross, cross, mine_z, sums_z, sum_send_z, sum_recv_z, lambda k: (slab, k), tuple)
        leaves = (leave_slab, leave_cross)
    whole = jnp.sum(whole, 1, keepdims=True)
    rz, zq, rw, qw, wv = (whole[k : k + 1] for k in range(5))
    alpha = rz / zq
    rz_new = rz - alpha * (zq + rw) + alpha * alpha * qw
    gain = 1.0 + rz_new / rz
    pq = gain * gain * zq - 2.0 * gain * alpha * qw + alpha * alpha * wv
    step = rz_new / pq
    of_z = alpha + step * gain
    of_w = -step * alpha
    x = of_z * z0 + of_w * w0

    def store(ref, value):
        ref[...] = jnp.concatenate([value[:64], value[64:]], 1)

    store(pot_ref, x)
    for part, (of_first, of_second) in enumerate(zip(*slopes)):
        store(vel_ref.at[part], of_z * of_first + of_w * of_second)

    for leave in leaves:
        leave()
    for turn_of in range(2):
        for side in range(4):
            @pl.when(sides[side][0])
            def _():
                face_copy(turn_of, side).wait_send()


def local(n_slab, n_cross, source, reaction, counts, orientation):
    slots, length = source.shape[1], source.shape[3]
    rows, lanes = slots * length, length * length
    first = n_slab * n_cross if n_slab * n_cross <= 64 else n_slab
    dma = pltpu.SemaphoreType.DMA
    vmem = pl.BlockSpec(memory_space=pltpu.VMEM)
    hbm = pl.BlockSpec(memory_space=pltpu.HBM)
    potential, velocity = pl.pallas_call(
        functools.partial(kernel, n_slab, n_cross),
        out_shape=(
            jax.ShapeDtypeStruct((rows, lanes), jnp.float32),
            jax.ShapeDtypeStruct((3, rows, lanes), jnp.float32),
        ),
        in_specs=[hbm, hbm, hbm, hbm],
        out_specs=(vmem, vmem),
        scratch_shapes=[
            pltpu.SMEM(counts.shape, jnp.int32),
            pltpu.SMEM((slots,), jnp.int32),
            pltpu.VMEM((rows, lanes), jnp.float32),
            pltpu.VMEM((rows, lanes), jnp.float32),
            dma((4,)),
            pltpu.VMEM((2, 4, 8, 128), jnp.float32),
            pltpu.VMEM((2, 4, 8, 128), jnp.float32),
            dma((2, 4)),
            dma((2, 4)),
            pltpu.VMEM((8, 128), jnp.float32),
            pltpu.VMEM((first, 8, 128), jnp.float32),
            dma((first,)),
            dma((first,)),
            pltpu.VMEM((8, 128), jnp.float32),
            pltpu.VMEM((n_cross, 8, 128), jnp.float32),
            dma((n_cross,)),
            dma((n_cross,)),
        ],
        compiler_params=pltpu.CompilerParams(
            collective_id=0, has_side_effects=True, vmem_limit_bytes=16 * 2**20
        ),
    )(
        *(
            pltpu.with_memory_space_constraint(x, pltpu.HBM)
            for x in (counts, orientation.reshape(slots), source.reshape(rows, lanes), reaction.reshape(rows, lanes))
        )
    )
    return potential.reshape(source.shape), velocity.reshape((3,) + source.shape)


def solution(mesh):
    spec = P("slab", None, "cross", None, None)
    return jax.shard_map(
        functools.partial(local, mesh.shape["slab"], mesh.shape["cross"]),
        mesh=mesh,
        in_specs=(spec, spec, P(), P("slab", None, "cross")),
        out_specs=(spec, P(None, "slab", None, "cross", None, None)),
        check_vma=False,
    )
```

```python
import functools

import jax
import jax.numpy as jnp
from jax import lax
from jax.experimental import pallas as pl
from jax.experimental.pallas import tpu as pltpu
from jax.sharding import PartitionSpec as P

LEVELS = 4
SWEEPS = 4
DAMPING = 0.8
KEEP = 1.0 - DAMPING


def roll(x, shift, axis):
    return pltpu.roll(x, shift % x.shape[axis], axis)


def iota(shape, axis):
    return lax.broadcasted_iota(jnp.int32, shape, axis)


def keep(mask, x):
    return jnp.where(mask, x, 0.0)


class Grid:
    def __init__(self):
        self.u = iota((128, 128), 0) % 16
        self.w = iota((128, 128), 1) % 16
        self.g = iota((64, 128), 1) // 16
        self.gg = iota((128, 128), 1) // 16

    def shifts(self, x, d):
        prev_u = keep(self.u >= d, roll(x, d, 0))
        next_u = keep(self.u < 16 - d, roll(x, -d, 0))
        prev_w = keep(self.w >= d, roll(x, d, 1))
        next_w = keep(self.w < 16 - d, roll(x, -d, 1))
        up = roll(x, 16 * d, 1)
        down = roll(x, -16 * d, 1)
        inside = self.g >= d
        prev_v = jnp.concatenate([keep(inside, up[:64]), jnp.where(inside, up[64:], up[:64])], 0)
        inside = self.g < 8 - d
        next_v = jnp.concatenate([jnp.where(inside, down[:64], down[64:]), keep(inside, down[64:])], 0)
        return prev_u, next_u, prev_v, next_v, prev_w, next_w

    def near(self, x, d):
        if d == 8:
            swap_u = x.reshape(8, 2, 8, 128)
            swap_u = jnp.concatenate([swap_u[:, 1:], swap_u[:, :1]], 1).reshape(128, 128)
            swap_v = jnp.concatenate([x[64:], x[:64]], 0)
            swap_w = jnp.where(self.w >= 8, roll(x, 8, 1), roll(x, -8, 1))
            return swap_u + swap_v + swap_w
        prev_u, next_u, prev_v, next_v, prev_w, next_w = self.shifts(x, d)
        return (prev_u + next_u) + (prev_v + next_v) + (prev_w + next_w)

    def restrict(self, x, d):
        x = x + jnp.where((self.u & d) != 0, roll(x, d, 0), roll(x, -d, 0))
        if d == 4:
            x = x + roll(x, 64, 1)
        else:
            x = x + jnp.where((self.gg & d) != 0, roll(x, 16 * d, 1), roll(x, -16 * d, 1))
        x = x + jnp.where((self.w & d) != 0, roll(x, d, 1), roll(x, -d, 1))
        return x * 0.125


def vcycle(grid, f, inverse, level):
    d = 2**level
    scale = 4.0**-level
    inv = inverse[level]
    e = inv * f
    if level == LEVELS - 1:
        for _ in range(SWEEPS - 1):
            e = KEEP * e + inv * (f + scale * grid.near(e, d))
        return e
    e = e + vcycle(grid, grid.restrict(KEEP * f + scale * grid.near(e, d), d), inverse, level + 1)
    return KEEP * e + inv * (f + scale * grid.near(e, d))


def fold(x):
    return x.reshape(8, 8, 128).sum(1)


def unfold(x):
    return jnp.broadcast_to(x[:, None, :], (8, 8, 128)).reshape(64, 128)


def spread(x):
    x = x + roll(x, 16, 1)
    x = x + roll(x, 32, 1)
    return x + roll(x, 64, 1)


def flip(x):
    row = iota(x.shape, 0)
    group = iota(x.shape, 1) // 16
    x = jnp.where(row % 2 == 1, roll(x, 1, 0), roll(x, -1, 0))
    x = roll(x, 64, 1)
    x = jnp.where((group & 2) != 0, roll(x, 32, 1), roll(x, -32, 1))
    return jnp.where((group & 1) != 0, roll(x, 16, 1), roll(x, -16, 1))


def pick(turn, a, b, c, d):
    return jnp.where(turn == 0, a, jnp.where(turn == 1, b, jnp.where(turn == 2, c, d)))


def kernel(
    n_slab, n_cross, counts_hbm, turn_hbm, source_hbm, reaction_hbm, pot_ref, vel_ref,
    counts_ref, turn_ref, source_ref, reaction_ref, load_sem,
    out_face, in_face, face_send, face_recv, mine, sums, sum_send, sum_recv,
    mine_z, sums_z, sum_send_z, sum_recv_z,
):
    slab = lax.axis_index("slab")
    cross = lax.axis_index("cross")

    loads = []
    pairs = ((counts_hbm, counts_ref), (reaction_hbm, reaction_ref), (turn_hbm, turn_ref), (source_hbm, source_ref))
    for place, (there, here) in enumerate(pairs):
        loads.append(pltpu.make_async_copy(there, here, load_sem.at[place]))
        loads[-1].start()

    in_face[...] = jnp.zeros_like(in_face)
    barrier = pltpu.get_barrier_semaphore()

    def each(count, body):
        if count <= 32:
            for step in range(1, count):
                body(step)
        else:
            lax.fori_loop(1, count, lambda step, carry: (body(step), carry)[1], 0)

    def greet_slab(step):
        pl.semaphore_signal(barrier, inc=1, device_id=(lax.rem(slab + step, n_slab), cross), device_id_type=pl.DeviceIdType.MESH)

    def greet_cross(step):
        pl.semaphore_signal(barrier, inc=1, device_id=(slab, lax.rem(cross + step, n_cross)), device_id_type=pl.DeviceIdType.MESH)

    devices = n_slab * n_cross
    direct = devices <= 64
    me = slab * n_cross + cross

    def seat(k):
        return k // n_cross, lax.rem(k, n_cross)

    def greet(step):
        pl.semaphore_signal(barrier, inc=1, device_id=seat(lax.rem(me + step, devices)), device_id_type=pl.DeviceIdType.MESH)

    if direct:
        each(devices, greet)
    else:
        each(n_slab, greet_slab)
        each(n_cross, greet_cross)

    grid = Grid()
    for each_load in loads:
        each_load.wait()
    live = counts_ref[slab]
    row8 = iota((8, 128), 0)
    turn = jnp.where(row8 < 2, turn_ref[0], jnp.where(row8 < 4, turn_ref[1], jnp.where(row8 < 6, turn_ref[2], turn_ref[3])))
    alive = (iota((128, 128), 0) % 64) // 16 < live
    u64 = grid.u[:64]
    diagonal_face = u64 % 8 == grid.g

    def load(ref):
        x = ref[...]
        return jnp.concatenate([x[:, :128], x[:, 128:]], 0)

    r0 = keep(alive, load(source_ref))
    coef = jnp.where(alive, load(reaction_ref), 1.0)
    inverse = []
    level_coef = coef
    for level in range(LEVELS):
        inverse.append(DAMPING / (6.0 * 4.0**-level + level_coef))
        if level + 1 < LEVELS:
            level_coef = grid.restrict(level_coef, 2**level)

    def faces(x):
        lo, hi = x[:64], x[64:]
        u0 = fold(keep(u64 == 0, lo)) + roll(fold(keep(u64 == 0, hi)), 1, 0)
        u1 = roll(fold(keep(u64 == 15, lo)), -1, 0) + fold(keep(u64 == 15, hi))
        v0 = fold(keep(diagonal_face, spread(keep(grid.g == 0, lo))))
        v1 = fold(keep(diagonal_face, spread(keep(grid.g == 7, hi))))
        flipped = flip(jnp.concatenate([u0, u1, v0, v1], 0))
        fu0, fu1, fv0, fv1 = flipped[:8], flipped[8:16], flipped[16:24], flipped[24:]
        return (
            pick(turn, u0, v1, fu1, fv0),
            pick(turn, u1, v0, fu0, fv1),
            pick(turn, v0, fu0, fv1, u1),
            pick(turn, v1, fu1, fv0, u0),
        )

    sides = (
        (slab + 1 < n_slab, slab > 0, (slab + 1, cross)),
        (slab > 0, slab + 1 < n_slab, (slab - 1, cross)),
        (cross + 1 < n_cross, cross > 0, (slab, cross + 1)),
        (cross > 0, cross + 1 < n_cross, (slab, cross - 1)),
    )

    def face_copy(turn_of, side):
        return pltpu.make_async_remote_copy(
            src_ref=out_face.at[turn_of, side],
            dst_ref=in_face.at[turn_of, side],
            send_sem=face_send.at[turn_of, side],
            recv_sem=face_recv.at[turn_of, side],
            device_id=sides[side][2],
            device_id_type=pl.DeviceIdType.MESH,
        )

    def exchange_start(turn_of, x):
        x0, x1, y0, y1 = faces(x)
        last = jnp.where(live == 1, x1, jnp.where(live == 2, roll(x1, -2, 0), jnp.where(live == 3, roll(x1, -4, 0), roll(x1, -6, 0))))
        out_face[turn_of, 0] = last
        out_face[turn_of, 1] = x0
        out_face[turn_of, 2] = y1
        out_face[turn_of, 3] = y0
        for side in range(4):
            @pl.when(sides[side][0])
            def _():
                face_copy(turn_of, side).start()
        return x0, x1

    def exchange_end(turn_of, x0, x1):
        for side in range(4):
            @pl.when(sides[side][1])
            def _():
                face_copy(turn_of, side).wait_recv()
        right = keep(row8 < 2, in_face[turn_of, 1])
        right = right + roll(right, 2, 0)
        right = right + roll(right, 4, 0)
        gx0 = jnp.where(row8 < 2, in_face[turn_of, 0], roll(x1, 2, 0))
        gx1 = jnp.where(row8 < 2 * (live - 1), roll(x0, -2, 0), right)
        gy0 = in_face[turn_of, 2]
        gy1 = in_face[turn_of, 3]
        flipped = flip(jnp.concatenate([gx0, gx1, gy0, gy1], 0))
        fx0, fx1, fy0, fy1 = flipped[:8], flipped[8:16], flipped[16:24], flipped[24:]
        gu0 = pick(turn, gx0, fy0, fx1, gy1)
        gu1 = pick(turn, gx1, fy1, fx0, gy0)
        gv0 = pick(turn, gy0, gx1, fy1, fx0)
        gv1 = pick(turn, gy1, gx0, fy0, fx1)
        lo = jnp.where(u64 == 0, unfold(gu0), keep(u64 == 15, unfold(roll(gu1, 1, 0))))
        hi = jnp.where(u64 == 0, unfold(roll(gu0, -1, 0)), keep(u64 == 15, unfold(gu1)))
        rim_u = jnp.concatenate([lo, hi], 0)
        lo = keep(grid.g == 0, spread(keep(diagonal_face, unfold(gv0))))
        hi = keep(grid.g == 7, spread(keep(diagonal_face, unfold(gv1))))
        rim_v = jnp.concatenate([lo, hi], 0)
        return rim_u, rim_v

    def interior(x):
        prev_u, next_u, prev_v, next_v, prev_w, next_w = grid.shifts(x, 1)
        image = (6.0 + coef) * x - ((prev_u + next_u) + (prev_v + next_v) + (prev_w + next_w))
        return image, next_u - prev_u, next_v - prev_v, keep(alive, 0.5 * (next_w - prev_w))

    def gradient(inside, rim_u, rim_v):
        along_u = inside[1] + jnp.where(grid.u == 0, -rim_u, rim_u)
        along_v = inside[2] + jnp.concatenate([-rim_v[:64], rim_v[64:]], 0)
        return keep(alive, 0.5 * along_u), keep(alive, 0.5 * along_v), inside[3]

    def inner(a, b):
        return (a * b).reshape(16, 8, 128).sum(0)

    z0 = vcycle(grid, r0, inverse, 0)
    pl.semaphore_wait(barrier, devices - 1 if direct else n_slab - 1 + n_cross - 1)
    z_faces = exchange_start(0, z0)
    dot_rz = inner(r0, z0)
    z_inside = interior(z0)
    z_rims = exchange_end(0, *z_faces)
    q0 = keep(alive, z_inside[0] - (z_rims[0] + z_rims[1]))
    w0 = vcycle(grid, q0, inverse, 0)
    w_faces = exchange_start(1, w0)
    dot_zq = inner(z0, q0)
    dot_rw = inner(r0, w0)
    dot_qw = inner(q0, w0)
    w_inside = interior(w0)
    w_rims = exchange_end(1, *w_faces)
    dot_wv = inner(w0, w_inside[0] - (w_rims[0] + w_rims[1]))
    none = jnp.zeros((8, 128), jnp.float32)
    partial = jnp.concatenate([dot_rz, dot_zq, dot_rw, dot_qw, dot_wv, none, none, none], 0)
    partial = jnp.sum(partial.reshape(8, 8, 128).sum(1), 1, keepdims=True)
    partial = jnp.sum(keep(iota((8, 128), 1) == row8, partial), 0, keepdims=True)

    def total(value, count, me, out, into, send, recv, place, beside):
        out[...] = value

        def copy(source, target):
            return pltpu.make_async_remote_copy(
                src_ref=out, dst_ref=into.at[source], send_sem=send.at[target], recv_sem=recv.at[source],
                device_id=place(target), device_id_type=pl.DeviceIdType.MESH,
            )

        def begin(step):
            copy(me, lax.rem(me + step, count)).start()

        def arrive(step):
            copy(lax.rem(me + step, count), lax.rem(me + step, count)).wait_recv()

        def leave(step):
            copy(me, lax.rem(me + step, count)).wait_send()

        each(count, begin)
        meanwhile = beside()
        into[me] = value
        each(count, arrive)
        result = into[...].sum(0)
        return result, meanwhile, lambda: each(count, leave)

    def gradients():
        return gradient(z_inside, *z_rims), gradient(w_inside, *w_rims)

    if direct:
        whole, slopes, leave = total(partial, devices, me, mine, sums, sum_send, sum_recv, seat, gradients)
        leaves = (leave,)
    else:
        across, slopes, leave_slab = total(partial, n_slab, slab, mine, sums, sum_send, sum_recv, lambda k: (k, cross), gradients)
        whole, _, leave_cross = total(across, n_cross, cross, mine_z, sums_z, sum_send_z, sum_recv_z, lambda k: (slab, k), tuple)
        leaves = (leave_slab, leave_cross)
    rz, zq, rw, qw, wv = (whole[:, k : k + 1] for k in range(5))
    alpha = rz / zq
    rz_new = rz - alpha * (zq + rw) + alpha * alpha * qw
    gain = 1.0 + rz_new / rz
    pq = gain * gain * zq - 2.0 * gain * alpha * qw + alpha * alpha * wv
    step = rz_new / pq
    of_z = alpha + step * gain
    of_w = -step * alpha
    x = of_z * z0 + of_w * w0

    def store(ref, value):
        ref[...] = jnp.concatenate([value[:64], value[64:]], 1)

    store(pot_ref, x)
    for part, (of_first, of_second) in enumerate(zip(*slopes)):
        store(vel_ref.at[part], of_z * of_first + of_w * of_second)

    for leave in leaves:
        leave()
    for turn_of in range(2):
        for side in range(4):
            @pl.when(sides[side][0])
            def _():
                face_copy(turn_of, side).wait_send()


def local(n_slab, n_cross, source, reaction, counts, orientation):
    slots, length = source.shape[1], source.shape[3]
    rows, lanes = slots * length, length * length
    first = n_slab * n_cross if n_slab * n_cross <= 64 else n_slab
    dma = pltpu.SemaphoreType.DMA
    vmem = pl.BlockSpec(memory_space=pltpu.VMEM)
    hbm = pl.BlockSpec(memory_space=pltpu.HBM)
    potential, velocity = pl.pallas_call(
        functools.partial(kernel, n_slab, n_cross),
        out_shape=(
            jax.ShapeDtypeStruct((rows, lanes), jnp.float32),
            jax.ShapeDtypeStruct((3, rows, lanes), jnp.float32),
        ),
        in_specs=[hbm, hbm, hbm, hbm],
        out_specs=(vmem, vmem),
        scratch_shapes=[
            pltpu.SMEM(counts.shape, jnp.int32),
            pltpu.SMEM((slots,), jnp.int32),
            pltpu.VMEM((rows, lanes), jnp.float32),
            pltpu.VMEM((rows, lanes), jnp.float32),
            dma((4,)),
            pltpu.VMEM((2, 4, 8, 128), jnp.float32),
            pltpu.VMEM((2, 4, 8, 128), jnp.float32),
            dma((2, 4)),
            dma((2, 4)),
            pltpu.VMEM((1, 128), jnp.float32),
            pltpu.VMEM((first, 1, 128), jnp.float32),
            dma((first,)),
            dma((first,)),
            pltpu.VMEM((1, 128), jnp.float32),
            pltpu.VMEM((n_cross, 1, 128), jnp.float32),
            dma((n_cross,)),
            dma((n_cross,)),
        ],
        compiler_params=pltpu.CompilerParams(
            collective_id=0, has_side_effects=True, vmem_limit_bytes=16 * 2**20
        ),
    )(
        *(
            pltpu.with_memory_space_constraint(x, pltpu.HBM)
            for x in (counts, orientation.reshape(slots), source.reshape(rows, lanes), reaction.reshape(rows, lanes))
        )
    )
    return potential.reshape(source.shape), velocity.reshape((3,) + source.shape)


def solution(mesh):
    spec = P("slab", None, "cross", None, None)
    return jax.shard_map(
        functools.partial(local, mesh.shape["slab"], mesh.shape["cross"]),
        mesh=mesh,
        in_specs=(spec, spec, P(), P("slab", None, "cross")),
        out_specs=(spec, P(None, "slab", None, "cross", None, None)),
        check_vma=False,
    )
```
